32 devices in a mesh: row: 8 (over z, y), col: 4 (over x, core).
Axes of the slice: x: 2, y: 2, z: 4, core: 2. Of those that a mesh axis runs over, the one named last changes fastest.
Arguments:
- operator: bfloat16 [32768, 32768], P('row', 'col'), may hold values from -0.0068359375 to 0.0068359375
- rhs: float32 [32, 32768], P(None, 'row'), may hold values from -72 to 72
- bodies: int32 [32768], P('row'), may hold values from 0 to 63, as said below
- weights: float32 [32768], P('row'), may hold values from 0.5 to 1.5
Outputs:
- basis: float32 [128, 32768], P(None, ('row', 'col'))
- hess: float32 [128, 96], replicated
- start_factor: float32 [32, 32], replicated
The draws below stay inside these ranges and needn't reach their ends.
Inputs may be any that keep to these rules, and one draw needn't show every extreme that they name: Every one of the 64 bodies has at least one node.
All inputs are finite; a program needn't handle non-finite values.
Results may differ from the reference program's by a relative error of at most 0.0025.
Values may be sent and summed in bfloat16 or wider, within the bound.
No kernel may reach another device: no remote copies, remote signals or barrier semaphores. Data moves between devices by JAX's collectives and lax.ppermute only.
A program may use at most 128 MiB of HBM per device.

```python
import jax
import jax.numpy as jnp
from jax import lax

N = 32768
S = 32
BODIES = 64
STEPS = 3


def body_index_of(key):
    position = jnp.arange(N, dtype=jnp.int32)
    random_ids = jax.random.randint(jax.random.fold_in(key, 11), (N,), 0, BODIES, dtype=jnp.int32)
    ordered = jnp.where(position < BODIES, position, random_ids)
    return jax.random.permutation(jax.random.fold_in(key, 12), ordered).astype(jnp.int32)


def draw_bodies(key, part):
    return body_index_of(key)


def draw_rhs(key, part):
    body_index = body_index_of(key)
    position = jnp.arange(N, dtype=jnp.float32)
    rigid_motion = jnp.clip(jax.random.normal(jax.random.fold_in(key, 21), (S, BODIES), jnp.float32), -4.0, 4.0)
    noise_part = jnp.clip(jax.random.normal(jax.random.fold_in(key, 22), (S, N), jnp.float32), -4.0, 4.0)
    amplitude = 1.0 + 3.0 * position / N
    values = amplitude[None, :] * (rigid_motion[:, body_index] + noise_part)
    return values.astype(jnp.float32)


def shard_levels(stream_key, dims, cuts, smallest, largest):
    factor_of = 1.0
    for axis_at, shards_of in cuts:
        steps = jax.random.uniform(jax.random.fold_in(jax.random.fold_in(stream_key, 6), axis_at), (shards_of,), jnp.float32, smallest / len(cuts), largest / len(cuts))
        factor_of = factor_of * jnp.repeat(jnp.exp(steps), dims[axis_at] // shards_of).reshape((-1,) + (1,) * (len(dims) - 1 - axis_at))
    return factor_of


def noise(rng, dims, spread, reach, cuts=(), kind=jnp.bfloat16):
    level = shard_levels(rng, dims, cuts, -0.22, 0.18) if cuts else 1.0
    array = jax.random.normal(rng, dims, jnp.float32) * spread * level
    return jnp.minimum(jnp.maximum(array, -reach), reach).astype(kind)


def setup_inputs(seed: int = 0) -> dict:
    key_of = jax.random.split(jax.random.key(seed), 5)
    operator = noise(key_of[0], (N, N), (25 * N) ** -0.5, 0.0068359375, ((0, 8), (1, 4)))
    rhs = draw_rhs(jax.random.fold_in(key_of[4], 71), 0)
    bodies = draw_bodies(jax.random.fold_in(key_of[4], 71), 0)
    weights = jnp.clip(1.0 + 0.1 * jax.random.normal(key_of[3], (N,), jnp.float32), 0.5, 1.5)
    return {"operator": operator, "rhs": rhs, "bodies": bodies, "weights": weights}


def product_t(left, right):
    return lax.dot_general(left.astype(jnp.float32), right.astype(jnp.float32), (((1,), (1,)), ((), ())), precision=lax.Precision.HIGHEST, preferred_element_type=jnp.float32)

def image_of(current, operator, onehot, weights):
    current_low = current.astype(jnp.bfloat16)
    block_rows = min(N, 2048)
    op_blocks = operator.reshape(N // block_rows, block_rows, N)

    def apply_rows(op_rows):
        return lax.dot_general(current_low.astype(jnp.float32), op_rows.astype(jnp.float32), (((1,), (1,)), ((), ())), preferred_element_type=jnp.float32)
    coupled = lax.map(apply_rows, op_blocks)
    coupled = jnp.transpose(coupled, (1, 0, 2)).reshape(current.shape[0], N)
    scaled = current_low.astype(jnp.float32) * weights[None, :]
    body_means = jnp.dot(scaled, onehot, precision=lax.Precision.HIGHEST) * (BODIES / N)
    completion = weights[None, :] * product_t(body_means, onehot)
    return 0.5 * current + coupled + completion

def reference(operator, rhs, bodies, weights):
    onehot = (bodies[:, None] == jnp.arange(BODIES, dtype=jnp.int32)[None, :]).astype(jnp.float32)
    gram_start = product_t(rhs, rhs) / N
    start_low = jnp.linalg.cholesky(gram_start)
    basis_list = [lax.linalg.triangular_solve(start_low, rhs, left_side=True, lower=True)]
    columns = []
    for step_index in range(STEPS):
        stacked = jnp.concatenate(basis_list, axis=0)
        image_block = image_of(basis_list[-1], operator, onehot, weights)
        first_coef = product_t(stacked, image_block) / N
        residual_one = image_block - jnp.dot(first_coef.T, stacked, precision=lax.Precision.HIGHEST)
        gram_block = product_t(residual_one, residual_one) / N
        factor_low = jnp.linalg.cholesky(gram_block)
        basis_list.append(lax.linalg.triangular_solve(factor_low, residual_one, left_side=True, lower=True))
        pieces = [first_coef, factor_low.T]
        below = (STEPS - 1 - step_index) * S
        if below > 0:
            pieces.append(jnp.zeros((below, S), jnp.float32))
        columns.append(jnp.concatenate(pieces, axis=0))
    return (jnp.concatenate(basis_list, axis=0), jnp.concatenate(columns, axis=1), start_low)
```

```python
import functools

import jax
import jax.numpy as jnp
from jax import lax
from jax.experimental import pallas as pl
from jax.experimental.pallas import tpu as pltpu
from jax.sharding import PartitionSpec as P

BODIES = 64
STEPS = 3
AXES = ("row", "col")
LANES = 128
EXTRA = 16
ROWS_A_COPY = 128
VMEM = pltpu.CompilerParams(vmem_limit_bytes=48 * 1024 * 1024)
f32 = jnp.float32
bf16 = jnp.bfloat16


def dot(left, right, left_dim, right_dim):
    return lax.dot_general(
        left, right, (((left_dim,), (right_dim,)), ((), ())), preferred_element_type=f32
    )


def dot_exact(left, right, left_dim, right_dim):
    return lax.dot_general(
        left,
        right,
        (((left_dim,), (right_dim,)), ((), ())),
        precision=lax.Precision.HIGHEST,
        preferred_element_type=f32,
    )


def split(value):
    high = value.astype(bf16)
    return high, (value - high.astype(f32)).astype(bf16)


def product_kernel(slots, group, q, x_ref, k_hbm, o_ref, buf, sem):
    t = buf.shape[0] // slots
    steps = k_hbm.shape[0] // t

    def copy(i, s):
        return pltpu.make_async_copy(
            k_hbm.at[pl.ds(pl.multiple_of(i * t, t), t)],
            buf.at[pl.ds(pl.multiple_of(s * t, t), t)],
            sem.at[s],
        )

    for i in range(min(slots, steps)):
        copy(i, i).start()
    x = x_ref[: o_ref.shape[1], : k_hbm.shape[1]]
    wide = t * group

    def step(i, carry):
        first = lax.rem(i * group, slots)
        for p in range(group):
            copy(i * group + p, first + p).wait()
        block = buf[pl.ds(pl.multiple_of(first * t, t), wide)]
        value = dot(block, x, 1, 1).T
        at = i * wide
        quarter = at // q
        place = (quarter // 2) * q + lax.rem(at, q)
        o_ref[lax.rem(quarter, 2), :, pl.ds(pl.multiple_of(place, LANES), wide)] = value

        @pl.when(i * group + slots < steps)
        def _():
            for p in range(group):
                copy(i * group + slots + p, first + p).start()

        return carry

    lax.fori_loop(0, steps // group, step, 0)


def product(x, s, operator, q):
    rows, width = operator.shape
    t = min(ROWS_A_COPY, q)
    group = max(1, min(4, q // t))
    slots = group * max(1, min(4, rows // (t * group)))
    return pl.pallas_call(
        functools.partial(product_kernel, slots, group, q),
        in_specs=[
            pl.BlockSpec(memory_space=pltpu.VMEM),
            pl.BlockSpec(memory_space=pl.ANY),
        ],
        out_specs=pl.BlockSpec(memory_space=pltpu.VMEM),
        out_shape=jax.ShapeDtypeStruct((2, s, rows // 2), f32),
        scratch_shapes=[
            pltpu.VMEM((slots * t, width), bf16),
            pltpu.SemaphoreType.DMA((slots,)),
        ],
        compiler_params=VMEM,
        cost_estimate=pl.CostEstimate(
            flops=2 * s * rows * width, bytes_accessed=2 * rows * width, transcendentals=0
        ),
        name="product",
    )(x, operator)


def gram_kernel(count, q, first, n_basis, *refs):
    refs = list(refs)
    off_ref = refs.pop(0)
    piece_refs = [refs.pop(0) for _ in range(count)]
    own_ref, weight_ref, body_ref = refs.pop(0), refs.pop(0), refs.pop(0)
    mean_ref = None if first else refs.pop(0)
    basis_refs = [refs.pop(0) for _ in range(n_basis)]
    w_ref, gram_ref = refs.pop(0), refs.pop(0)
    if first:
        weight_out, body_out = refs.pop(0), refs.pop(0)
    s = own_ref.shape[0]
    end = w_ref.shape[1] - q
    if not first:
        m_high, m_rest = split(mean_ref[...])
        m_rest32 = mean_ref[...] - m_high.astype(f32)
        m_low = (m_rest32 - m_rest.astype(f32)).astype(bf16)
        means = jnp.concatenate([m_high, m_rest, m_low], axis=0)
        body_row = lax.broadcasted_iota(jnp.int32, (BODIES, q), 0)

    def place(value, weight, body, at):
        if not first:
            onehot = (body_row == body).astype(f32).astype(bf16)
            picked = dot(means, onehot, 1, 0)
            value = value + weight * (picked[:s] + picked[s : 2 * s] + picked[2 * s :])
        high, low = split(value)
        w_ref[:s, pl.ds(at, q)] = high
        w_ref[s:, pl.ds(at, q)] = low

    k = 0
    for ref in piece_refs:
        for d in range(ref.shape[0]):
            at = pl.multiple_of(off_ref[k], LANES)
            k += 1
            codes = ref[d].astype(jnp.int32).astype(f32)
            scale = jnp.exp2(codes[:s, q : q + 1] * 0.125)
            value = codes[:s, :q] * scale
            if first:
                weight = (codes[s : s + 1, :q] + codes[s + 1 : s + 2, :q] * 2.0**-15) * 2.0**-14
                body = codes[s + 2 : s + 3, :q].astype(jnp.int32)
                weight_out[:, pl.ds(at, q)] = weight
                body_out[:, pl.ds(at, q)] = body
            else:
                weight = weight_ref[:, pl.ds(at, q)]
                body = body_ref[:, pl.ds(at, q)]
            place(value, weight, body, at)
    if first:
        weight_out[:, end:] = weight_ref[...]
        body_out[:, end:] = body_ref[...]
        place(own_ref[...], None, None, end)
    else:
        place(own_ref[...], weight_ref[:, end:], body_ref[:, end:], end)
    span = slice(0, end) if count else slice(0, q)
    new = w_ref[:, span]
    blocks = [ref[:, span] for ref in basis_refs] + [new]
    raw = dot(jnp.concatenate(blocks, axis=0), new, 1, 1)
    for b in range(n_basis + 1):
        part = raw[2 * s * b : 2 * s * b + s] + raw[2 * s * b + s : 2 * s * (b + 1)]
        gram_ref[s * b : s * (b + 1), :] = part[:, :s] + part[:, s:]


def gram_call(offsets, pieces, own, weight, body, means, basis, first):
    s, q = own.shape
    n_basis = len(basis)
    wide = q
    for p in pieces:
        wide += p.shape[0] * q
    outs = [
        jax.ShapeDtypeStruct((2 * s, wide), bf16),
        jax.ShapeDtypeStruct((s * (n_basis + 1), s), f32),
    ]
    if first:
        outs += [
            jax.ShapeDtypeStruct((1, wide), f32),
            jax.ShapeDtypeStruct((1, wide), jnp.int32),
        ]
    args = [offsets, *pieces, own, weight, body]
    if not first:
        args.append(means)
    args += basis
    specs = [pl.BlockSpec(memory_space=pltpu.SMEM)]
    specs += [pl.BlockSpec(memory_space=pltpu.VMEM)] * (len(args) - 1)
    return pl.pallas_call(
        functools.partial(gram_kernel, len(pieces), q, first, n_basis),
        in_specs=specs,
        out_specs=[pl.BlockSpec(memory_space=pltpu.VMEM)] * len(outs),
        out_shape=outs,
        compiler_params=VMEM,
        name="gram",
    )(*args)


def factor(gram):
    n = gram.shape[0]
    row = lax.broadcasted_iota(jnp.int32, (n, n), 0)
    lane = lax.broadcasted_iota(jnp.int32, (n, n), 1)
    left, right = gram, (row == lane).astype(f32)
    for k in range(n):
        pivot = left[k : k + 1, k : k + 1]
        root = lax.rsqrt(pivot)
        root = root * (1.5 - 0.5 * pivot * root * root)
        left_row = left[k : k + 1, :] * root
        right_row = right[k : k + 1, :] * root
        column = jnp.where(row > k, left[:, k : k + 1] * root, 0.0)
        left = jnp.where(row == k, left_row, left - column * left_row)
        right = jnp.where(row == k, right_row, right - column * right_row)
    return jnp.where(lane >= row, left, 0.0), jnp.where(lane <= row, right, 0.0)


def next_kernel(n, q, n_basis, last, *refs):
    refs = list(refs)
    gram_ref, w_ref = refs.pop(0), refs.pop(0)
    basis_refs = [refs.pop(0) for _ in range(n_basis)]
    if not last:
        weight_ref, body_ref = refs.pop(0), refs.pop(0)
    own_ref, upper_ref = refs.pop(0), refs.pop(0)
    if n_basis:
        coef_ref = refs.pop(0)
    if not last:
        v_ref, mean_ref = refs.pop(0), refs.pop(0)
    s = own_ref.shape[0]
    gram = gram_ref[n_basis * s :, :] / n
    if n_basis:
        coef = gram_ref[: n_basis * s, :] / n
        gram = gram - dot_exact(coef, coef, 0, 0)
        row = lax.broadcasted_iota(jnp.int32, (n_basis * s, s), 0)
        lane = lax.broadcasted_iota(jnp.int32, (n_basis * s, s), 1)
        coef_ref[...] = coef + jnp.where(row == lane + (n_basis - 1) * s, 0.5, 0.0)
    upper, inverse = factor(gram)
    upper_ref[...] = upper
    high, low = split(inverse)
    mix = [jnp.concatenate([high, low], axis=0)] * 2
    for b in range(n_basis):
        high, low = split(-dot_exact(inverse, coef[b * s : (b + 1) * s], 1, 1))
        mix += [jnp.concatenate([high, low], axis=0)] * 2
    mix = jnp.concatenate(mix, axis=1)
    wide = w_ref.shape[1]
    if not last:
        body_row = lax.broadcasted_iota(jnp.int32, (BODIES, q), 0)
        means = jnp.zeros((2 * s, BODIES), f32)
    for at in range(0, wide, q):
        span = slice(at, at + q)
        stack = jnp.concatenate([w_ref[:, span]] + [r[:, span] for r in basis_refs], axis=0)
        both = dot(mix, stack, 1, 0)
        value = both[:s] + both[s:]
        if at == wide - q:
            own_ref[...] = value
        if not last:
            high, low = split(value)
            v_ref[:s, span] = high
            v_ref[s:, span] = low
            if at < wide - q:
                onehot = (body_row == body_ref[:, span]).astype(f32).astype(bf16)
                u_high, u_low = split(high.astype(f32) * weight_ref[:, span])
                means = means + dot(jnp.concatenate([u_high, u_low], axis=0), onehot, 1, 1)
    if not last:
        mean_ref[...] = (means[:s] + means[s:]) * (BODIES / n)


def next_call(n, q, gram, w, basis, weight, body, last):
    s = gram.shape[1]
    n_basis = len(basis)
    outs = [jax.ShapeDtypeStruct((s, q), f32), jax.ShapeDtypeStruct((s, s), f32)]
    if n_basis:
        outs.append(jax.ShapeDtypeStruct((n_basis * s, s), f32))
    args = [gram, w, *basis]
    if not last:
        outs += [
            jax.ShapeDtypeStruct(w.shape, bf16),
            jax.ShapeDtypeStruct((s, BODIES), f32),
        ]
        args += [weight, body]
    return pl.pallas_call(
        functools.partial(next_kernel, n, q, n_basis, last),
        in_specs=[pl.BlockSpec(memory_space=pltpu.VMEM)] * len(args),
        out_specs=[pl.BlockSpec(memory_space=pltpu.VMEM)] * len(outs),
        out_shape=outs,
        compiler_params=VMEM,
        name="next_block",
    )(*args)


def encode(value):
    largest = jnp.maximum(jnp.max(jnp.abs(value), axis=1, keepdims=True), 1e-30)
    level = jnp.ceil(8.0 * jnp.log2(largest / 32000.0))
    codes = jnp.round(value / jnp.exp2(level * 0.125))
    levels = jnp.broadcast_to(level, (value.shape[0], LANES))
    return jnp.concatenate([codes, levels], axis=1).astype(jnp.int16)


def local(rows, cols, operator, rhs, bodies, weights):
    row_index, col_index = lax.axis_index("row"), lax.axis_index("col")
    s, block = rhs.shape
    n = block * rows
    q = block // cols
    span = rows // cols
    plane, inner = row_index // span, lax.rem(row_index, span)
    width = operator.shape[1]

    def index(a, g, c):
        return (a * span + g) * cols + c

    places = [(a, g, c) for a in range(cols) for g in range(span) for c in range(cols)]

    def permute(value, to):
        return lax.ppermute(value, AXES, [(index(*p), index(*to(*p))) for p in places])

    def gather(payload):
        rounds = [
            permute(payload, lambda a, g, c, d=d: ((c + d) % cols, g, a)) for d in range(cols)
        ]
        mine = jnp.stack(rounds)
        return [mine] + [
            permute(mine, lambda a, g, c, d=d: (a, (g + d) % span, c)) for d in range(1, span)
        ]

    offsets = jnp.stack(
        [
            lax.rem(inner - d + span, span) * block + lax.rem(plane - e + cols, cols) * q
            for d in range(span)
            for e in range(cols)
        ]
    ).astype(jnp.int32)

    def sum_cols(value):
        bit = 1
        while bit < cols:
            value = value + permute(value, lambda a, g, c, bit=bit: (a, g, c ^ bit))
            bit *= 2
        return value

    def sum_all(value):
        value = sum_cols(value)
        bit = 1
        while bit < span:
            value = value + permute(value, lambda a, g, c, bit=bit: (a, g ^ bit, c))
            bit *= 2
        bit = 1
        while bit < cols:
            value = value + permute(value, lambda a, g, c, bit=bit: (a ^ bit, g, c))
            bit *= 2
        return value

    def scatter_cols(partial):
        core = lax.rem(col_index, 2)
        keep = lax.dynamic_index_in_dim(partial, core, 0, False)
        send = lax.dynamic_index_in_dim(partial, 1 - core, 0, False)
        value = keep + permute(send, lambda a, g, c: (a, g, c ^ 1))
        bit = cols // 2
        while bit > 1:
            half = value.shape[1] // 2
            side = lax.rem(col_index // bit, 2)
            keep = lax.dynamic_slice_in_dim(value, side * half, half, 1)
            send = lax.dynamic_slice_in_dim(value, (1 - side) * half, half, 1)
            value = keep + permute(send, lambda a, g, c, bit=bit: (a, g, c ^ bit))
            bit //= 2
        return value

    own_rhs = lax.dynamic_slice_in_dim(rhs, col_index * q, q, 1)
    own_weight = lax.dynamic_slice_in_dim(weights, col_index * q, q, 0)[None, :]
    own_body = lax.dynamic_slice_in_dim(bodies, col_index * q, q, 0)[None, :]
    weight_scaled = own_weight * 2.0**14
    weight_high = jnp.round(weight_scaled)
    weight_low = jnp.round((weight_scaled - weight_high) * 2.0**15)
    extra = jnp.concatenate(
        [
            weight_high,
            weight_low,
            own_body.astype(f32),
            jnp.zeros((EXTRA - 3, q), f32),
        ],
        axis=0,
    ).astype(jnp.int16)
    extra = jnp.pad(extra, ((0, 0), (0, LANES)))
    payload = jnp.concatenate([encode(own_rhs), extra], axis=0)
    w, gram, weight, body = gram_call(
        offsets, gather(payload), own_rhs, own_weight, own_body, None, [], True
    )
    own, start_upper, v, means = next_call(n, q, sum_cols(gram), w, [], weight, body, False)
    basis, owns, columns = [v], [own], []
    for step in range(STEPS):
        last = step == STEPS - 1
        means = sum_cols(means)
        partial = product(basis[-1], s, operator, q)
        coupled = scatter_cols(partial)
        if last:
            own_basis = [b[:, width:] for b in basis]
            w, gram = gram_call(
                offsets, [], coupled, own_weight, own_body, means, own_basis, False
            )
            own, upper, coef = next_call(
                n, q, sum_all(gram), w, own_basis, None, None, True
            )
        else:
            w, gram = gram_call(
                offsets, gather(encode(coupled)), coupled, weight, body, means, basis, False
            )
            own, upper, coef, v, means = next_call(
                n, q, sum_cols(gram), w, basis, weight, body, False
            )
            basis.append(v)
        owns.append(own)
        pieces = [coef, upper]
        below = (STEPS - 1 - step) * s
        if below > 0:
            pieces.append(jnp.zeros((below, s), f32))
        columns.append(jnp.concatenate(pieces, axis=0))
    return (jnp.concatenate(owns, axis=0), jnp.concatenate(columns, axis=1), start_upper.T)


def solution(mesh):
    rows, cols = mesh.shape["row"], mesh.shape["col"]
    in_specs = (P("row", "col"), P(None, "row"), P("row"), P("row"))
    out_specs = (P(None, ("row", "col")), P(), P())
    return jax.shard_map(
        functools.partial(local, rows, cols),
        mesh=mesh,
        in_specs=in_specs,
        out_specs=out_specs,
        check_vma=False,
    )
```

```python
import functools

import jax
import jax.numpy as jnp
from jax import lax
from jax.experimental import pallas as pl
from jax.experimental.pallas import tpu as pltpu
from jax.sharding import PartitionSpec as P

BODIES = 64
STEPS = 3
AXES = ("row", "col")
LANES = 128
EXTRA = 16
PARAMS = pltpu.CompilerParams(vmem_limit_bytes=48 * 1024 * 1024)
f32 = jnp.float32
bf16 = jnp.bfloat16
i16 = jnp.int16
i32 = jnp.int32


def dot(left, right, left_dim, right_dim):
    return lax.dot_general(
        left, right, (((left_dim,), (right_dim,)), ((), ())), preferred_element_type=f32
    )


def dot_exact(left, right, left_dim, right_dim):
    return lax.dot_general(
        left,
        right,
        (((left_dim,), (right_dim,)), ((), ())),
        precision=lax.Precision.HIGHEST,
        preferred_element_type=f32,
    )


def split(value):
    high = value.astype(bf16)
    return high, (value - high.astype(f32)).astype(bf16)


def onehot_of(body):
    row = lax.broadcasted_iota(i32, (BODIES, body.shape[1]), 0)
    return (row == body).astype(f32)


def padded(width):
    return -(-width // LANES) * LANES


def level_of(value):
    largest = jnp.maximum(jnp.max(jnp.abs(value), axis=1, keepdims=True), 1e-30)
    return jnp.ceil(8.0 * jnp.log2(largest * (1.0 / 32000.0)))


def write_payload(ref, value, sums):
    s, q = value.shape
    level = level_of(value)
    ref[:s, :q] = jnp.round(value / jnp.exp2(level * 0.125)).astype(i32).astype(i16)
    sum_level = level_of(sums)
    scaled = sums / jnp.exp2(sum_level * 0.125)
    high = jnp.round(scaled)
    low = jnp.round((scaled - high) * 2.0**15)
    k = sums.shape[1]
    rest = ref.shape[1] - q - 2 * k
    lane = lax.broadcasted_iota(i32, (s, rest), 1)
    levels = jnp.where(lane == 0, level, jnp.where(lane == 1, sum_level, 0.0))
    ref[:s, q:] = jnp.concatenate([high, low, levels], axis=1).astype(i32).astype(i16)


def read_sums(tail, k):
    scale = jnp.exp2(tail[:, 2 * k + 1 : 2 * k + 2] * 0.125)
    return (tail[:, :k] + tail[:, k : 2 * k] * 2.0**-15) * scale


def payload_width(q, k):
    return q + padded(2 * k + 2)


def start_kernel(at_ref, rhs_ref, weight_ref, body_ref, own_ref, w_ref, b_ref, payload_ref):
    s, q = own_ref.shape
    at = pl.multiple_of(at_ref[0], LANES)
    own = rhs_ref[:, pl.ds(at, q)]
    weight = weight_ref[:, pl.ds(at, q)]
    body = body_ref[:, pl.ds(at, q)]
    own_ref[...] = own
    w_ref[...] = weight
    b_ref[...] = body
    bodies = onehot_of(body) * weight
    sums = dot_exact(own, jnp.concatenate([own, bodies], axis=0), 1, 1)
    write_payload(payload_ref, own, sums)
    scaled = weight * 2.0**14
    high = jnp.round(scaled)
    low = jnp.round((scaled - high) * 2.0**15)
    row = lax.broadcasted_iota(i32, (EXTRA, q), 0)
    extra = jnp.where(row == 0, high, jnp.where(row == 1, low, 0.0))
    extra = jnp.where(row == 2, body.astype(f32), extra)
    payload_ref[s:, :q] = extra.astype(i32).astype(i16)
    payload_ref[s:, q:] = jnp.zeros((EXTRA, payload_ref.shape[1] - q), i16)


def start_call(at, rhs, weights, bodies, q):
    s = rhs.shape[0]
    k = s + BODIES
    vmem = pl.BlockSpec(memory_space=pltpu.VMEM)
    return pl.pallas_call(
        start_kernel,
        in_specs=[pl.BlockSpec(memory_space=pltpu.SMEM), vmem, vmem, vmem],
        out_specs=[vmem] * 4,
        out_shape=[
            jax.ShapeDtypeStruct((s, q), f32),
            jax.ShapeDtypeStruct((1, q), f32),
            jax.ShapeDtypeStruct((1, q), i32),
            jax.ShapeDtypeStruct((s + EXTRA, payload_width(q, k)), i16),
        ],
        compiler_params=PARAMS,
        name="start",
    )(at, rhs, weights, bodies)


def product_kernel(blocks, cols, slots, t, group, s, k, q, first, carry, *refs):
    refs = list(refs)
    place_ref = refs.pop(0)
    piece_refs = [refs.pop(0) for _ in blocks]
    if not first:
        weight_ref, body_ref, mean_ref = refs.pop(0), refs.pop(0), refs.pop(0)
    if carry:
        before_ref, sums_before_ref = refs.pop(0), refs.pop(0)
    k_hbm, o_ref, sums_ref = refs.pop(0), refs.pop(0), refs.pop(0)
    if first:
        weight_out, body_out = refs.pop(0), refs.pop(0)
    x_ref, buf, sem = refs
    block = cols * q
    wide = t * group
    steps = k_hbm.shape[0] // t

    def copies(i, slot):
        for b, d in enumerate(blocks):
            at = pl.multiple_of(place_ref[cols + d], LANES)
            yield pltpu.make_async_copy(
                k_hbm.at[pl.ds(pl.multiple_of(i * t, t), t), pl.ds(at, block)],
                buf.at[pl.ds(pl.multiple_of(slot * t, t), t), pl.ds(b * block, block)],
                sem.at[slot, b],
            )

    for i in range(min(slots, steps)):
        for copy in copies(i, i):
            copy.start()

    if not first:
        means = mean_ref[...]
        m_high, m_mid = split(means)
        m_low = (means - m_high.astype(f32) - m_mid.astype(f32)).astype(bf16)
        means = jnp.concatenate([m_high, m_mid, m_low], axis=0)
    total = jnp.zeros((s, k), f32)
    for b in range(len(blocks)):
        for e in range(cols):
            at = b * block + pl.multiple_of(place_ref[e], LANES)
            codes = piece_refs[b][e].astype(i32).astype(f32)
            tail = codes[:s, q:]
            total = total + read_sums(tail, k)
            value = codes[:s, :q] * jnp.exp2(tail[:, 2 * k : 2 * k + 1] * 0.125)
            if first:
                weight = codes[s : s + 1, :q] + codes[s + 1 : s + 2, :q] * 2.0**-15
                weight_out[:, pl.ds(at, q)] = weight * 2.0**-14
                body_out[:, pl.ds(at, q)] = codes[s + 2 : s + 3, :q].astype(i32)
            else:
                onehot = onehot_of(body_ref[:, pl.ds(at, q)]).astype(bf16)
                picked = dot(means, onehot, 1, 0)
                picked = picked[:s] + picked[s : 2 * s] + picked[2 * s :]
                value = value + weight_ref[:, pl.ds(at, q)] * picked
            high, low = split(value)
            x_ref[:s, pl.ds(at, q)] = high
            x_ref[s:, pl.ds(at, q)] = low
    if carry:
        total = total + sums_before_ref[...][:, :k]
    rest = sums_ref.shape[1] - k
    if rest:
        total = jnp.concatenate([total, jnp.zeros((s, rest), f32)], axis=1)
    sums_ref[...] = total

    def step(i, state):
        slot = lax.rem(i * group, slots)
        for p in range(group):
            for copy in copies(i * group + p, slot + p):
                copy.wait()
        rows = buf[pl.ds(pl.multiple_of(slot * t, t), wide)]
        both = dot(rows, x_ref[...], 1, 1).T
        value = both[:s] + both[s:]
        at = i * wide
        quarter = at // q
        place = pl.multiple_of((quarter // 2) * q + lax.rem(at, q), LANES)
        half = lax.rem(quarter, 2)
        if carry:
            value = value + before_ref[half, :, pl.ds(place, wide)]
        o_ref[half, :, pl.ds(place, wide)] = value

        @pl.when(i * group + slots < steps)
        def _():
            for p in range(group):
                for copy in copies(i * group + slots + p, slot + p):
                    copy.start()

        return state

    lax.fori_loop(0, steps // group, step, 0)


def product_call(blocks, places, pieces, s, k, q, cols, operator, near, before):
    rows = operator.shape[0]
    block = cols * q
    t = min(256, q)
    group = max(1, min(512, q) // t)
    slots = group * min(4, rows // (t * group))
    first = near is None
    vmem = pl.BlockSpec(memory_space=pltpu.VMEM)
    args = [places, *pieces]
    specs = [pl.BlockSpec(memory_space=pltpu.SMEM)] + [vmem] * len(pieces)
    if not first:
        args += near
        specs += [vmem] * 3
    if before is not None:
        args += before
        specs += [vmem] * 2
    args.append(operator)
    specs.append(pl.BlockSpec(memory_space=pl.ANY))
    wide = block * len(blocks)
    outs = [
        jax.ShapeDtypeStruct((2, s, rows // 2), f32),
        jax.ShapeDtypeStruct((s, padded(k)), f32),
    ]
    if first:
        outs += [jax.ShapeDtypeStruct((1, wide), f32), jax.ShapeDtypeStruct((1, wide), i32)]
    return pl.pallas_call(
        functools.partial(
            product_kernel, blocks, cols, slots, t, group, s, k, q, first, before is not None
        ),
        in_specs=specs,
        out_specs=[vmem] * len(outs),
        out_shape=outs,
        scratch_shapes=[
            pltpu.VMEM((2 * s, wide), bf16),
            pltpu.VMEM((slots * t, wide), bf16),
            pltpu.SemaphoreType.DMA((slots, len(blocks))),
        ],
        compiler_params=PARAMS,
        cost_estimate=pl.CostEstimate(
            flops=4 * s * rows * wide, bytes_accessed=2 * rows * wide, transcendentals=0
        ),
        name="product",
    )(*args)


def factor(gram):
    n = gram.shape[0]
    row = lax.broadcasted_iota(i32, (n, n), 0)
    lane = lax.broadcasted_iota(i32, (n, n), 1)
    left, right = gram, (row == lane).astype(f32)
    for k in range(n):
        pivot = left[k : k + 1, k : k + 1]
        root = lax.rsqrt(pivot)
        root = root * (1.5 - 0.5 * pivot * root * root)
        left_row = left[k : k + 1, :] * root
        right_row = right[k : k + 1, :] * root
        column = jnp.where(row > k, left[:, k : k + 1] * root, 0.0)
        left = jnp.where(row == k, left_row, left - column * left_row)
        right = jnp.where(row == k, right_row, right - column * right_row)
    return jnp.where(lane >= row, left, 0.0), jnp.where(lane <= row, right, 0.0)


def next_kernel(n, n_basis, kind, *refs):
    refs = list(refs)
    sums_ref, new_ref = refs.pop(0), refs.pop(0)
    basis_refs = [refs.pop(0) for _ in range(n_basis)]
    if kind != "last":
        image_ref, weight_ref, body_ref = refs.pop(0), refs.pop(0), refs.pop(0)
        image_refs = [refs.pop(0) for _ in range(n_basis)]
        mass_refs = [refs.pop(0) for _ in range(n_basis)]
    v_ref, upper_ref = refs.pop(0), refs.pop(0)
    if n_basis:
        coef_ref = refs.pop(0)
    s, q = v_ref.shape
    k = n_basis * s
    gram = sums_ref[:, k : k + s] / n
    if n_basis:
        coef = sums_ref[:, :k] / n
        gram = gram - dot_exact(coef, coef, 1, 1)
        row = lax.broadcasted_iota(i32, (k, s), 0)
        lane = lax.broadcasted_iota(i32, (k, s), 1)
        coef_ref[...] = coef.T + jnp.where(row == lane + (k - s), 0.5, 0.0)
    upper, inverse = factor(gram)
    upper_ref[...] = upper
    mix = inverse
    if n_basis:
        mix = jnp.concatenate([inverse, -dot_exact(inverse, coef, 1, 0)], axis=1)

    def mixed(values):
        return dot_exact(mix, jnp.concatenate(values, axis=0), 1, 0)

    v = mixed([new_ref[...]] + [r[...] for r in basis_refs])
    v_ref[...] = v
    if kind == "last":
        return
    y = mixed([image_ref[...]] + [r[...] for r in image_refs])
    mass = mixed([sums_ref[:, k + s : k + s + BODIES]] + [r[...] for r in mass_refs])
    onehot = onehot_of(body_ref[...])
    weight = weight_ref[...]
    means = mass * (BODIES / n)
    w = y + weight * dot_exact(means, onehot, 1, 0)
    stack = [r[...] for r in basis_refs] + [v, w]
    if kind == "middle":
        y_ref, w_ref, mass_ref, mean_ref, payload_ref = refs
        y_ref[...] = y
        mass_ref[...] = mass
        mean_ref[...] = means
        sums = dot_exact(w, jnp.concatenate(stack + [onehot * weight], axis=0), 1, 1)
        write_payload(payload_ref, y, sums)
    else:
        w_ref, sums_out = refs
        sums_out[...] = dot_exact(w, jnp.concatenate(stack, axis=0), 1, 1)
    w_ref[...] = w


def next_call(n, kind, sums, new, basis, image=None, weight=None, body=None, images=(), masses=()):
    s, q = new.shape
    n_basis = len(basis)
    args = [sums, new, *basis]
    if kind != "last":
        args += [image, weight, body, *images, *masses]
    outs = [jax.ShapeDtypeStruct((s, q), f32), jax.ShapeDtypeStruct((s, s), f32)]
    if n_basis:
        outs.append(jax.ShapeDtypeStruct((n_basis * s, s), f32))
    if kind == "middle":
        k = (n_basis + 2) * s + BODIES
        outs += [jax.ShapeDtypeStruct((s, q), f32)] * 2
        outs += [jax.ShapeDtypeStruct((s, BODIES), f32)] * 2
        outs.append(jax.ShapeDtypeStruct((s, payload_width(q, k)), i16))
    elif kind == "before last":
        outs.append(jax.ShapeDtypeStruct((s, q), f32))
        outs.append(jax.ShapeDtypeStruct((s, (n_basis + 2) * s), f32))
    vmem = pl.BlockSpec(memory_space=pltpu.VMEM)
    return pl.pallas_call(
        functools.partial(next_kernel, n, n_basis, kind),
        in_specs=[vmem] * len(args),
        out_specs=[vmem] * len(outs),
        out_shape=outs,
        compiler_params=PARAMS,
        name="next_block",
    )(*args)


def local(rows, cols, operator, rhs, bodies, weights):
    row_index, col_index = lax.axis_index("row"), lax.axis_index("col")
    s, block = rhs.shape
    n = block * rows
    q = block // cols
    span = rows // cols
    plane, inner = row_index // span, lax.rem(row_index, span)
    places = [(a, g, c) for a in range(cols) for g in range(span) for c in range(cols)]

    def index(a, g, c):
        return (a * span + g) * cols + c

    def permute(value, to):
        return lax.ppermute(value, AXES, [(index(*p), index(*to(*p))) for p in places])

    offsets = jnp.stack(
        [lax.rem(plane - e + cols, cols) * q for e in range(cols)]
        + [lax.rem(inner - d + span, span) * block for d in range(span)]
    ).astype(i32)

    def sum_all(value):
        for bit in [1 << b for b in range(cols.bit_length() - 1)]:
            value = value + permute(value, lambda a, g, c: (a, g, c ^ bit))
        for bit in [1 << b for b in range(span.bit_length() - 1)]:
            value = value + permute(value, lambda a, g, c: (a, g ^ bit, c))
        for bit in [1 << b for b in range(cols.bit_length() - 1)]:
            value = value + permute(value, lambda a, g, c: (a ^ bit, g, c))
        return value

    def scatter_cols(partial, sums):
        core = lax.rem(col_index, 2)
        keep = lax.dynamic_index_in_dim(partial, core, 0, False)
        send = lax.dynamic_index_in_dim(partial, 1 - core, 0, False)
        moved = permute(jnp.concatenate([send, sums], axis=1), lambda a, g, c: (a, g, c ^ 1))
        value = keep + moved[:, : keep.shape[1]]
        sums = sums + moved[:, keep.shape[1] :]
        bit = cols // 2
        while bit > 1:
            half = value.shape[1] // 2
            side = lax.rem(col_index // bit, 2)
            keep = lax.dynamic_slice_in_dim(value, side * half, half, 1)
            send = lax.dynamic_slice_in_dim(value, (1 - side) * half, half, 1)
            moved = permute(
                jnp.concatenate([send, sums], axis=1), lambda a, g, c, bit=bit: (a, g, c ^ bit)
            )
            value = keep + moved[:, :half]
            sums = sums + moved[:, half:]
            bit //= 2
        return value, sums

    def image(payload, k, near):
        rounds = [
            permute(payload, lambda a, g, c, d=d: ((c + d) % cols, g, a)) for d in range(cols)
        ]
        mine = jnp.stack(rounds)
        others = [
            permute(mine, lambda a, g, c, d=d: (a, (g + d) % span, c)) for d in range(1, span)
        ]
        first = near is None
        part = product_call(
            (0,), offsets, [mine], s, k, q, cols, operator, None if first else near[0], None
        )
        rest = product_call(
            tuple(range(1, span)),
            offsets,
            others,
            s,
            k,
            q,
            cols,
            operator,
            None if first else near[1],
            part[:2],
        )
        value, sums = scatter_cols(rest[0], rest[1])
        return value, sums, (part[2:], rest[2:])

    new, own_weight, own_body, payload = start_call(
        (col_index * q).astype(i32).reshape(1), rhs, weights[None, :], bodies[None, :], q
    )
    k = s + BODIES
    basis, images, masses, columns = [], [], [], []
    near = None
    for step in range(STEPS):
        value, sums, found = image(payload, k, near)
        if step == 0:
            around = found
        kind = "middle" if step < STEPS - 1 else "before last"
        out = next_call(
            n, kind, sums, new, basis, value, own_weight, own_body, images, masses
        )
        basis.append(out[0])
        columns.append(out[1 : 2 + min(step, 1)])
        if kind == "middle":
            y, new, mass, means, payload = out[-5:]
            images.append(y)
            masses.append(mass)
            near = [[*a, means] for a in around]
            k = (step + 2) * s + BODIES
        else:
            new, sums = out[-2:]
    out = next_call(n, "last", sum_all(sums), new, basis)
    basis.append(out[0])
    columns.append(out[1:])
    hess = []
    for step, (upper, coef) in enumerate(columns[1:]):
        below = (STEPS - 1 - step) * s
        hess.append(jnp.pad(jnp.concatenate([coef, upper], axis=0), ((0, below), (0, 0))))
    return (
        jnp.concatenate(basis, axis=0),
        jnp.concatenate(hess, axis=1),
        columns[0][0].T,
    )


def solution(mesh):
    rows, cols = mesh.shape["row"], mesh.shape["col"]
    in_specs = (P("row", "col"), P(None, "row"), P("row"), P("row"))
    out_specs = (P(None, ("row", "col")), P(), P())
    return jax.shard_map(
        functools.partial(local, rows, cols),
        mesh=mesh,
        in_specs=in_specs,
        out_specs=out_specs,
        check_vma=False,
    )
```

```python
import functools

import jax
import jax.numpy as jnp
from jax import lax
from jax.experimental import pallas as pl
from jax.experimental.pallas import tpu as pltpu
from jax.sharding import PartitionSpec as P

BODIES = 64
STEPS = 3
AXES = ("row", "col")
LANES = 128
EXTRA = 8
PARAMS = pltpu.CompilerParams(vmem_limit_bytes=48 * 1024 * 1024)
f32 = jnp.float32
bf16 = jnp.bfloat16
i16 = jnp.int16
i32 = jnp.int32


def dot(left, right, left_dim, right_dim):
    return lax.dot_general(
        left, right, (((left_dim,), (right_dim,)), ((), ())), preferred_element_type=f32
    )


def dot_exact(left, right, left_dim, right_dim):
    return lax.dot_general(
        left,
        right,
        (((left_dim,), (right_dim,)), ((), ())),
        precision=lax.Precision.HIGHEST,
        preferred_element_type=f32,
    )


def split(value):
    high = value.astype(bf16)
    return high, (value - high.astype(f32)).astype(bf16)


def onehot_of(body):
    row = lax.broadcasted_iota(i32, (BODIES, body.shape[1]), 0)
    return (row == body).astype(f32)


def padded(width):
    return -(-width // LANES) * LANES


def level_of(value):
    largest = jnp.maximum(jnp.max(jnp.abs(value), axis=1, keepdims=True), 1e-30)
    return jnp.ceil(8.0 * jnp.log2(largest * (1.0 / 32000.0)))


def write_payload(ref, value, sums, extra=None):
    s, q = value.shape
    k = sums.shape[1] - BODIES
    level = level_of(value)
    codes = jnp.round(value / jnp.exp2(level * 0.125))
    inner = sums[:, :k]
    inner_level = level_of(inner)
    scaled = inner / jnp.exp2(inner_level * 0.125)
    high = jnp.round(scaled)
    low = jnp.round((scaled[:, k - s :] - high[:, k - s :]) * 2.0**15)
    mass = sums[:, k:]
    mass_level = level_of(mass)
    mass_codes = jnp.round(mass / jnp.exp2(mass_level * 0.125))
    rest = ref.shape[1] - q - k - s - BODIES
    lane = lax.broadcasted_iota(i32, (s, rest), 1)
    levels = jnp.where(lane == 1, inner_level, jnp.where(lane == 2, mass_level, 0.0))
    levels = jnp.where(lane == 0, level, levels)
    tail = jnp.concatenate([high, low, mass_codes, levels], axis=1)
    if extra is not None:
        codes = jnp.concatenate([codes, extra], axis=0)
        below = jnp.zeros((extra.shape[0], tail.shape[1]), f32)
        tail = jnp.concatenate([tail, below], axis=0)
    ref[:, :q] = codes.astype(i32).astype(i16)
    ref[:, q:] = tail.astype(i32).astype(i16)


def read_sums(tail, k):
    s = tail.shape[0]
    k = k - BODIES
    at = k + s + BODIES
    low = jnp.concatenate([jnp.zeros((s, k - s), f32), tail[:, k : k + s]], axis=1) if k > s else tail[:, k : k + s]
    inner = (tail[:, :k] + low * 2.0**-15) * jnp.exp2(tail[:, at + 1 : at + 2] * 0.125)
    mass = tail[:, k + s : at] * jnp.exp2(tail[:, at + 2 : at + 3] * 0.125)
    return jnp.concatenate([inner, mass], axis=1)


def payload_width(q, k, s):
    return q + padded(k + s + 3)


def start_kernel(at_ref, rhs_hbm, weight_hbm, body_hbm, own_ref, w_ref, b_ref, payload_ref, sem):
    s, q = own_ref.shape
    at = pl.multiple_of(at_ref[0], LANES)
    pairs = ((rhs_hbm, own_ref), (weight_hbm, w_ref), (body_hbm, b_ref))
    copies = [
        pltpu.make_async_copy(src.at[:, pl.ds(at, q)], dst, sem.at[i])
        for i, (src, dst) in enumerate(pairs)
    ]
    for copy in copies:
        copy.start()
    for copy in copies:
        copy.wait()
    own, weight, body = own_ref[...], w_ref[...], b_ref[...]
    bodies = onehot_of(body) * weight
    sums = dot_exact(own, jnp.concatenate([own, bodies], axis=0), 1, 1)
    scaled = weight * 2.0**14
    high = jnp.round(scaled)
    low = jnp.round((scaled - high) * 2.0**15)
    row = lax.broadcasted_iota(i32, (EXTRA, q), 0)
    extra = jnp.where(row == 0, high, jnp.where(row == 1, low, 0.0))
    extra = jnp.where(row == 2, body.astype(f32), extra)
    write_payload(payload_ref, own, sums, extra)


def start_call(at, rhs, weights, bodies, q):
    s = rhs.shape[0]
    k = s + BODIES
    vmem = pl.BlockSpec(memory_space=pltpu.VMEM)
    return pl.pallas_call(
        start_kernel,
        in_specs=[pl.BlockSpec(memory_space=pltpu.SMEM)] + [pl.BlockSpec(memory_space=pl.ANY)] * 3,
        out_specs=[vmem] * 4,
        scratch_shapes=[pltpu.SemaphoreType.DMA((3,))],
        out_shape=[
            jax.ShapeDtypeStruct((s, q), f32),
            jax.ShapeDtypeStruct((1, q), f32),
            jax.ShapeDtypeStruct((1, q), i32),
            jax.ShapeDtypeStruct((s + EXTRA, payload_width(q, k, s)), i16),
        ],
        compiler_params=pltpu.CompilerParams(vmem_limit_bytes=63 * 1024 * 1024),
        name="start",
    )(at, rhs, weights, bodies)


def product_kernel(blocks, cols, slots, t, group, s, k, q, first, carry, *refs):
    refs = list(refs)
    place_ref = refs.pop(0)
    piece_refs = [refs.pop(0) for _ in blocks]
    if not first:
        weight_ref, body_ref, mean_ref = refs.pop(0), refs.pop(0), refs.pop(0)
    if carry:
        before_ref, sums_before_ref = refs.pop(0), refs.pop(0)
    k_hbm, o_ref, sums_ref = refs.pop(0), refs.pop(0), refs.pop(0)
    if first:
        weight_out, body_out = refs.pop(0), refs.pop(0)
    x_ref, buf, sem = refs
    block = cols * q
    wide = t * group
    steps = k_hbm.shape[0] // t

    def copies(i, slot):
        for b, d in enumerate(blocks):
            at = pl.multiple_of(place_ref[cols + d], LANES)
            yield pltpu.make_async_copy(
                k_hbm.at[pl.ds(pl.multiple_of(i * t, t), t), pl.ds(at, block)],
                buf.at[pl.ds(pl.multiple_of(slot * t, t), t), pl.ds(b * block, block)],
                sem.at[slot, b],
            )

    for i in range(min(slots, steps)):
        for copy in copies(i, i):
            copy.start()

    if not first:
        means = mean_ref[...]
        m_high, m_mid = split(means)
        m_low = (means - m_high.astype(f32) - m_mid.astype(f32)).astype(bf16)
        means = jnp.concatenate([m_high, m_mid, m_low], axis=0)
    total = jnp.zeros((s, k), f32)
    for b in range(len(blocks)):
        for e in range(cols):
            at = b * block + pl.multiple_of(place_ref[e], LANES)
            codes = piece_refs[b][e].astype(i32).astype(f32)
            tail = codes[:s, q:]
            total = total + read_sums(tail, k)
            value = codes[:s, :q] * jnp.exp2(tail[:, k + s : k + s + 1] * 0.125)
            if first:
                weight = codes[s : s + 1, :q] + codes[s + 1 : s + 2, :q] * 2.0**-15
                weight_out[:, pl.ds(at, q)] = weight * 2.0**-14
                body_out[:, pl.ds(at, q)] = codes[s + 2 : s + 3, :q].astype(i32)
            else:
                onehot = onehot_of(body_ref[:, pl.ds(at, q)]).astype(bf16)
                picked = dot(means, onehot, 1, 0)
                picked = picked[:s] + picked[s : 2 * s] + picked[2 * s :]
                value = value + weight_ref[:, pl.ds(at, q)] * picked
            high, low = split(value)
            x_ref[:s, pl.ds(at, q)] = high
            x_ref[s:, pl.ds(at, q)] = low
    if carry:
        total = total + sums_before_ref[...][:, :k]
    rest = sums_ref.shape[1] - k
    if rest:
        total = jnp.concatenate([total, jnp.zeros((s, rest), f32)], axis=1)
    sums_ref[...] = total

    def step(i, state):
        slot = lax.rem(i * group, slots)
        for p in range(group):
            for copy in copies(i * group + p, slot + p):
                copy.wait()
        rows = buf[pl.ds(pl.multiple_of(slot * t, t), wide)]
        both = dot(rows, x_ref[...], 1, 1).T
        value = both[:s] + both[s:]
        at = i * wide
        quarter = at // q
        place = pl.multiple_of((quarter // 2) * q + lax.rem(at, q), LANES)
        half = lax.rem(quarter, 2)
        if carry:
            value = value + before_ref[half, :, pl.ds(place, wide)]
        o_ref[half, :, pl.ds(place, wide)] = value

        @pl.when(i * group + slots < steps)
        def _():
            for p in range(group):
                for copy in copies(i * group + slots + p, slot + p):
                    copy.start()

        return state

    lax.fori_loop(0, steps // group, step, 0)


def product_call(blocks, places, pieces, s, k, q, cols, operator, near, before):
    rows = operator.shape[0]
    block = cols * q
    t = min(256, q)
    group = max(1, min(512, q) // t)
    slots = group * min(4, rows // (t * group))
    first = near is None
    vmem = pl.BlockSpec(memory_space=pltpu.VMEM)
    args = [places, *pieces]
    specs = [pl.BlockSpec(memory_space=pltpu.SMEM)] + [vmem] * len(pieces)
    if not first:
        args += near
        specs += [vmem] * 3
    if before is not None:
        args += before
        specs += [vmem] * 2
    args.append(operator)
    specs.append(pl.BlockSpec(memory_space=pl.ANY))
    wide = block * len(blocks)
    outs = [
        jax.ShapeDtypeStruct((2, s, rows // 2), f32),
        jax.ShapeDtypeStruct((s, padded(k)), f32),
    ]
    if first:
        outs += [jax.ShapeDtypeStruct((1, wide), f32), jax.ShapeDtypeStruct((1, wide), i32)]
    return pl.pallas_call(
        functools.partial(
            product_kernel, blocks, cols, slots, t, group, s, k, q, first, before is not None
        ),
        in_specs=specs,
        out_specs=[vmem] * len(outs),
        out_shape=outs,
        scratch_shapes=[
            pltpu.VMEM((2 * s, wide), bf16),
            pltpu.VMEM((slots * t, wide), bf16),
            pltpu.SemaphoreType.DMA((slots, len(blocks))),
        ],
        compiler_params=PARAMS,
        cost_estimate=pl.CostEstimate(
            flops=4 * s * rows * wide, bytes_accessed=2 * rows * wide, transcendentals=0
        ),
        name="product",
    )(*args)


def factor(gram):
    n = gram.shape[0]
    panel = 8
    row = lax.broadcasted_iota(i32, (n, 2 * n), 0)
    lane = lax.broadcasted_iota(i32, (n, 2 * n), 1)
    left = jnp.concatenate([gram, jnp.zeros_like(gram)], axis=1) + (lane == row + n).astype(f32)
    found, pivots = [], []
    for at in range(0, n, panel):
        height = n - at
        pivot = jnp.ones((panel, 2 * n), f32)
        for k in range(panel):
            column = jnp.broadcast_to(left[:, at + k : at + k + 1], (height, 2 * n))
            top = column[k : k + 1, :]
            pivot = jnp.where(row[:panel] == k, top, pivot)
            below = jnp.where(row[:height] > k, column, 0.0)
            left = left - below * (left[k : k + 1, :] * (1.0 / top))
        found.append(left[:panel])
        pivots.append(pivot)
        left = left[panel:]
    left, pivot = jnp.concatenate(found, axis=0), jnp.concatenate(pivots, axis=0)
    root = lax.rsqrt(pivot)
    left = left * (root * (1.5 - 0.5 * pivot * root * root))
    row, lane = row[:, :n], lane[:, :n]
    return jnp.where(lane >= row, left[:, :n], 0.0), jnp.where(lane <= row, left[:, n:], 0.0)


def next_kernel(n, n_basis, kind, *refs):
    refs = list(refs)
    sums_ref, new_ref = refs.pop(0), refs.pop(0)
    basis_refs = [refs.pop(0) for _ in range(n_basis)]
    if kind == "last":
        upper_refs = [refs.pop(0) for _ in range(n_basis)]
        coef_refs = [refs.pop(0) for _ in range(n_basis - 1)]
        out_ref, hess_ref, start_ref = refs
        s, q = new_ref.shape
    else:
        image_ref, weight_ref, body_ref = refs.pop(0), refs.pop(0), refs.pop(0)
        image_refs = [refs.pop(0) for _ in range(n_basis)]
        mass_refs = [refs.pop(0) for _ in range(n_basis)]
        v_ref, upper_ref = refs.pop(0), refs.pop(0)
        s, q = v_ref.shape
        if n_basis:
            coef_ref = refs.pop(0)
    k = n_basis * s
    gram = sums_ref[:, k : k + s] / n
    if n_basis:
        coef = sums_ref[:, :k] / n
        gram = gram - dot_exact(coef, coef, 1, 1)
        row = lax.broadcasted_iota(i32, (k, s), 0)
        lane = lax.broadcasted_iota(i32, (k, s), 1)
        shifted = coef.T + jnp.where(row == lane + (k - s), 0.5, 0.0)
        if kind != "last":
            coef_ref[...] = shifted
    upper, inverse = factor(gram)
    if kind != "last":
        upper_ref[...] = upper
    mix = inverse
    if n_basis:
        mix = jnp.concatenate([inverse, -dot_exact(inverse, coef, 1, 0)], axis=1)

    def mixed(values):
        return dot_exact(mix, jnp.concatenate(values, axis=0), 1, 0)

    v = mixed([new_ref[...]] + [r[...] for r in basis_refs])
    if kind == "last":
        for b, ref in enumerate(basis_refs):
            out_ref[b * s : (b + 1) * s, :] = ref[...]
        out_ref[n_basis * s :, :] = v
        hess = []
        for b in range(n_basis):
            blocks = [coef_refs[b][...] if b < n_basis - 1 else shifted]
            blocks.append(upper_refs[b + 1][...] if b < n_basis - 1 else upper)
            if b < n_basis - 1:
                blocks.append(jnp.zeros(((n_basis - 1 - b) * s, s), f32))
            hess.append(jnp.concatenate(blocks, axis=0))
        hess_ref[...] = jnp.concatenate(hess, axis=1)
        start_ref[...] = upper_refs[0][...].T
        return
    v_ref[...] = v
    y = mixed([image_ref[...]] + [r[...] for r in image_refs])
    mass = mixed([sums_ref[:, k + s : k + s + BODIES]] + [r[...] for r in mass_refs])
    onehot = onehot_of(body_ref[...])
    weight = weight_ref[...]
    means = mass * (BODIES / n)
    w = y + weight * dot_exact(means, onehot, 1, 0)
    stack = [r[...] for r in basis_refs] + [v, w]
    if kind == "middle":
        y_ref, w_ref, mass_ref, mean_ref, payload_ref = refs
        y_ref[...] = y
        mass_ref[...] = mass
        mean_ref[...] = means
        sums = dot_exact(w, jnp.concatenate(stack + [onehot * weight], axis=0), 1, 1)
        write_payload(payload_ref, y, sums)
    else:
        w_ref, sums_out = refs
        sums_out[...] = dot_exact(w, jnp.concatenate(stack, axis=0), 1, 1)
    w_ref[...] = w


def next_call(n, kind, sums, new, basis, *more):
    s, q = new.shape
    n_basis = len(basis)
    args = [sums, new, *basis, *more]
    if kind == "last":
        outs = [
            jax.ShapeDtypeStruct(((n_basis + 1) * s, q), f32),
            jax.ShapeDtypeStruct(((n_basis + 1) * s, n_basis * s), f32),
            jax.ShapeDtypeStruct((s, s), f32),
        ]
    else:
        outs = [jax.ShapeDtypeStruct((s, q), f32), jax.ShapeDtypeStruct((s, s), f32)]
        if n_basis:
            outs.append(jax.ShapeDtypeStruct((n_basis * s, s), f32))
    if kind == "middle":
        k = (n_basis + 2) * s + BODIES
        outs += [jax.ShapeDtypeStruct((s, q), f32)] * 2
        outs += [jax.ShapeDtypeStruct((s, BODIES), f32)] * 2
        outs.append(jax.ShapeDtypeStruct((s, payload_width(q, k, s)), i16))
    elif kind == "before last":
        outs.append(jax.ShapeDtypeStruct((s, q), f32))
        outs.append(jax.ShapeDtypeStruct((s, (n_basis + 2) * s), f32))
    vmem = pl.BlockSpec(memory_space=pltpu.VMEM)
    return pl.pallas_call(
        functools.partial(next_kernel, n, n_basis, kind),
        in_specs=[vmem] * len(args),
        out_specs=[vmem] * len(outs),
        out_shape=outs,
        compiler_params=PARAMS,
        name="next_block",
    )(*args)


def local(rows, cols, operator, rhs, bodies, weights):
    row_index, col_index = lax.axis_index("row"), lax.axis_index("col")
    s, block = rhs.shape
    n = block * rows
    q = block // cols
    span = rows // cols
    plane, inner = row_index // span, lax.rem(row_index, span)
    places = [(a, g, c) for a in range(cols) for g in range(span) for c in range(cols)]

    def index(a, g, c):
        return (a * span + g) * cols + c

    def permute(value, to):
        return lax.ppermute(value, AXES, [(index(*p), index(*to(*p))) for p in places])

    offsets = jnp.stack(
        [lax.rem(plane - e + cols, cols) * q for e in range(cols)]
        + [lax.rem(inner - d + span, span) * block for d in range(span)]
    ).astype(i32)

    def sum_all(value):
        for bit in [1 << b for b in range(cols.bit_length() - 1)]:
            value = value + permute(value, lambda a, g, c: (a, g, c ^ bit))
        for bit in [1 << b for b in range(span.bit_length() - 1)]:
            value = value + permute(value, lambda a, g, c: (a, g ^ bit, c))
        for bit in [1 << b for b in range(cols.bit_length() - 1)]:
            value = value + permute(value, lambda a, g, c: (a ^ bit, g, c))
        return value

    def scatter_cols(partial, sums):
        core = lax.rem(col_index, 2)
        keep = lax.dynamic_index_in_dim(partial, core, 0, False)
        send = lax.dynamic_index_in_dim(partial, 1 - core, 0, False)
        moved = permute(jnp.concatenate([send, sums], axis=1), lambda a, g, c: (a, g, c ^ 1))
        value = keep + moved[:, : keep.shape[1]]
        sums = sums + moved[:, keep.shape[1] :]
        bit = cols // 2
        while bit > 1:
            half = value.shape[1] // 2
            side = lax.rem(col_index // bit, 2)
            keep = lax.dynamic_slice_in_dim(value, side * half, half, 1)
            send = lax.dynamic_slice_in_dim(value, (1 - side) * half, half, 1)
            level = level_of(send)
            codes = jnp.round(send / jnp.exp2(level * 0.125))
            levels = jnp.broadcast_to(level, (s, LANES))
            codes = jnp.concatenate([codes, levels], axis=1).astype(i16)
            moved, more = [
                permute(v, lambda a, g, c, bit=bit: (a, g, c ^ bit)) for v in (codes, sums)
            ]
            scale = jnp.exp2(moved[:, half : half + 1].astype(f32) * 0.125)
            value = keep + moved[:, :half].astype(f32) * scale
            sums = sums + more
            bit //= 2
        return value, sums

    def image(payload, k, near):
        rounds = [
            permute(payload, lambda a, g, c, d=d: ((c + d) % cols, g, a)) for d in range(cols)
        ]
        mine = jnp.stack(rounds)
        others = [
            permute(mine, lambda a, g, c, d=d: (a, (g + d) % span, c)) for d in range(1, span)
        ]
        first = near is None
        part = product_call(
            (0,), offsets, [mine], s, k, q, cols, operator, None if first else near[0], None
        )
        rest = product_call(
            tuple(range(1, span)),
            offsets,
            others,
            s,
            k,
            q,
            cols,
            operator,
            None if first else near[1],
            part[:2],
        )
        value, sums = scatter_cols(rest[0], rest[1])
        return value, sums, (part[2:], rest[2:])

    new, own_weight, own_body, payload = start_call(
        (col_index * q).astype(i32).reshape(1), rhs, weights[None, :], bodies[None, :], q
    )
    k = s + BODIES
    basis, images, masses, uppers, coefs = [], [], [], [], []
    near = None
    for step in range(STEPS):
        value, sums, found = image(payload, k, near)
        if step == 0:
            around = found
        kind = "middle" if step < STEPS - 1 else "before last"
        out = list(
            next_call(n, kind, sums, new, basis, value, own_weight, own_body, *images, *masses)
        )
        basis.append(out.pop(0))
        uppers.append(out.pop(0))
        if step:
            coefs.append(out.pop(0))
        if kind == "middle":
            y, new, mass, means, payload = out
            images.append(y)
            masses.append(mass)
            near = [[*a, means] for a in around]
            k = (step + 2) * s + BODIES
        else:
            new, sums = out
    return tuple(next_call(n, "last", sum_all(sums), new, basis, *uppers, *coefs))


def solution(mesh):
    rows, cols = mesh.shape["row"], mesh.shape["col"]
    in_specs = (P("row", "col"), P(None, "row"), P("row"), P("row"))
    out_specs = (P(None, ("row", "col")), P(), P())
    return jax.shard_map(
        functools.partial(local, rows, cols),
        mesh=mesh,
        in_specs=in_specs,
        out_specs=out_specs,
        check_vma=False,
    )
```

```python
import functools

import jax
import jax.numpy as jnp
from jax import lax
from jax.experimental import pallas as pl
from jax.experimental.pallas import tpu as pltpu
from jax.sharding import PartitionSpec as P

BODIES = 64
STEPS = 3
AXES = ("row", "col")
LANES = 128
EXTRA = 8
PARAMS = pltpu.CompilerParams(vmem_limit_bytes=48 * 1024 * 1024)
f32 = jnp.float32
bf16 = jnp.bfloat16
i16 = jnp.int16
i32 = jnp.int32


def dot(left, right, left_dim, right_dim):
    return lax.dot_general(
        left, right, (((left_dim,), (right_dim,)), ((), ())), preferred_element_type=f32
    )


def dot_exact(left, right, left_dim, right_dim):
    return lax.dot_general(
        left,
        right,
        (((left_dim,), (right_dim,)), ((), ())),
        precision=lax.Precision.HIGHEST,
        preferred_element_type=f32,
    )


def split(value):
    high = value.astype(bf16)
    return high, (value - high.astype(f32)).astype(bf16)


def dot_close(left, right, left_dim, right_dim):
    left_high, left_low = split(left)
    right_high, right_low = split(right)
    rows = left.shape[0]
    both = dot(jnp.concatenate([left_high, left_low], axis=0), right_high, left_dim, right_dim)
    return both[:rows] + both[rows:] + dot(left_high, right_low, left_dim, right_dim)


def onehot_of(body):
    row = lax.broadcasted_iota(i32, (BODIES, body.shape[1]), 0)
    return (row == body).astype(f32)


def padded(width):
    return -(-width // LANES) * LANES


def level_of(value):
    largest = jnp.maximum(jnp.max(jnp.abs(value), axis=1, keepdims=True), 1e-30)
    return jnp.ceil(8.0 * jnp.log2(largest * (1.0 / 32000.0)))


def write_payload(ref, value, sums, extra=None):
    s, q = value.shape
    k = sums.shape[1] - BODIES
    level = level_of(value)
    codes = jnp.round(value / jnp.exp2(level * 0.125))
    inner = sums[:, :k]
    inner_level = level_of(inner)
    scaled = inner / jnp.exp2(inner_level * 0.125)
    high = jnp.round(scaled)
    low = jnp.round((scaled[:, k - s :] - high[:, k - s :]) * 2.0**15)
    mass = sums[:, k:]
    mass_level = level_of(mass)
    mass_codes = jnp.round(mass / jnp.exp2(mass_level * 0.125))
    rest = ref.shape[1] - q - k - s - BODIES
    lane = lax.broadcasted_iota(i32, (s, rest), 1)
    levels = jnp.where(lane == 1, inner_level, jnp.where(lane == 2, mass_level, 0.0))
    levels = jnp.where(lane == 0, level, levels)
    tail = jnp.concatenate([high, low, mass_codes, levels], axis=1)
    if extra is not None:
        codes = jnp.concatenate([codes, extra], axis=0)
        below = jnp.zeros((extra.shape[0], tail.shape[1]), f32)
        tail = jnp.concatenate([tail, below], axis=0)
    ref[:, :q] = codes.astype(i32).astype(i16)
    ref[:, q:] = tail.astype(i32).astype(i16)


def read_sums(tail, k):
    s = tail.shape[0]
    k = k - BODIES
    at = k + s + BODIES
    low = jnp.concatenate([jnp.zeros((s, k - s), f32), tail[:, k : k + s]], axis=1) if k > s else tail[:, k : k + s]
    inner = (tail[:, :k] + low * 2.0**-15) * jnp.exp2(tail[:, at + 1 : at + 2] * 0.125)
    mass = tail[:, k + s : at] * jnp.exp2(tail[:, at + 2 : at + 3] * 0.125)
    return jnp.concatenate([inner, mass], axis=1)


def payload_width(q, k, s):
    return q + padded(k + s + 3)


def start_kernel(at_ref, rhs_hbm, weight_hbm, body_hbm, own_ref, w_ref, b_ref, payload_ref, sem):
    s, q = own_ref.shape
    at = pl.multiple_of(at_ref[0], LANES)
    pairs = ((rhs_hbm, own_ref), (weight_hbm, w_ref), (body_hbm, b_ref))
    copies = [
        pltpu.make_async_copy(src.at[:, pl.ds(at, q)], dst, sem.at[i])
        for i, (src, dst) in enumerate(pairs)
    ]
    for copy in copies:
        copy.start()
    for copy in copies:
        copy.wait()
    own, weight, body = own_ref[...], w_ref[...], b_ref[...]
    bodies = onehot_of(body) * weight
    sums = dot_close(own, jnp.concatenate([own, bodies], axis=0), 1, 1)
    scaled = weight * 2.0**14
    high = jnp.round(scaled)
    low = jnp.round((scaled - high) * 2.0**15)
    row = lax.broadcasted_iota(i32, (EXTRA, q), 0)
    extra = jnp.where(row == 0, high, jnp.where(row == 1, low, 0.0))
    extra = jnp.where(row == 2, body.astype(f32), extra)
    write_payload(payload_ref, own, sums, extra)


def start_call(at, rhs, weights, bodies, q):
    s = rhs.shape[0]
    k = s + BODIES
    vmem = pl.BlockSpec(memory_space=pltpu.VMEM)
    return pl.pallas_call(
        start_kernel,
        in_specs=[pl.BlockSpec(memory_space=pltpu.SMEM)] + [pl.BlockSpec(memory_space=pl.ANY)] * 3,
        out_specs=[vmem] * 4,
        scratch_shapes=[pltpu.SemaphoreType.DMA((3,))],
        out_shape=[
            jax.ShapeDtypeStruct((s, q), f32),
            jax.ShapeDtypeStruct((1, q), f32),
            jax.ShapeDtypeStruct((1, q), i32),
            jax.ShapeDtypeStruct((s + EXTRA, payload_width(q, k, s)), i16),
        ],
        compiler_params=pltpu.CompilerParams(vmem_limit_bytes=63 * 1024 * 1024),
        name="start",
    )(at, rhs, weights, bodies)


def product_kernel(blocks, cols, slots, t, group, s, k, q, first, carry, *refs):
    refs = list(refs)
    place_ref = refs.pop(0)
    piece_refs = [refs.pop(0) for _ in blocks]
    if not first:
        weight_ref, body_ref, mean_ref = refs.pop(0), refs.pop(0), refs.pop(0)
    if carry:
        before_ref, sums_before_ref = refs.pop(0), refs.pop(0)
    k_hbm, o_ref, sums_ref = refs.pop(0), refs.pop(0), refs.pop(0)
    if first:
        weight_out, body_out = refs.pop(0), refs.pop(0)
    x_ref, buf, sem = refs
    block = cols * q
    wide = t * group
    steps = k_hbm.shape[0] // t

    def copies(i, slot):
        for b, d in enumerate(blocks):
            at = pl.multiple_of(place_ref[cols + d], LANES)
            yield pltpu.make_async_copy(
                k_hbm.at[pl.ds(pl.multiple_of(i * t, t), t), pl.ds(at, block)],
                buf.at[pl.ds(pl.multiple_of(slot * t, t), t), pl.ds(b * block, block)],
                sem.at[slot, b],
            )

    for i in range(min(slots, steps)):
        for copy in copies(i, i):
            copy.start()

    if not first:
        means = mean_ref[...]
        m_high, m_mid = split(means)
        m_low = (means - m_high.astype(f32) - m_mid.astype(f32)).astype(bf16)
        means = jnp.concatenate([m_high, m_mid, m_low], axis=0)
    total = jnp.zeros((s, k), f32)
    for b in range(len(blocks)):
        for e in range(cols):
            at = b * block + pl.multiple_of(place_ref[e], LANES)
            codes = piece_refs[b][e].astype(i32).astype(f32)
            tail = codes[:s, q:]
            total = total + read_sums(tail, k)
            value = codes[:s, :q] * jnp.exp2(tail[:, k + s : k + s + 1] * 0.125)
            if first:
                weight = codes[s : s + 1, :q] + codes[s + 1 : s + 2, :q] * 2.0**-15
                weight_out[:, pl.ds(at, q)] = weight * 2.0**-14
                body_out[:, pl.ds(at, q)] = codes[s + 2 : s + 3, :q].astype(i32)
            else:
                onehot = onehot_of(body_ref[:, pl.ds(at, q)]).astype(bf16)
                picked = dot(means, onehot, 1, 0)
                picked = picked[:s] + picked[s : 2 * s] + picked[2 * s :]
                value = value + weight_ref[:, pl.ds(at, q)] * picked
            high, low = split(value)
            x_ref[:s, pl.ds(at, q)] = high
            x_ref[s:, pl.ds(at, q)] = low
    if carry:
        total = total + sums_before_ref[...][:, :k]
    rest = sums_ref.shape[1] - k
    if rest:
        total = jnp.concatenate([total, jnp.zeros((s, rest), f32)], axis=1)
    sums_ref[...] = total

    def step(i, state):
        slot = lax.rem(i * group, slots)
        for p in range(group):
            for copy in copies(i * group + p, slot + p):
                copy.wait()
        rows = buf[pl.ds(pl.multiple_of(slot * t, t), wide)]
        both = dot(rows, x_ref[...], 1, 1).T
        value = both[:s] + both[s:]
        at = i * wide
        quarter = at // q
        place = pl.multiple_of((quarter // 2) * q + lax.rem(at, q), LANES)
        half = lax.rem(quarter, 2)
        if carry:
            value = value + before_ref[half, :, pl.ds(place, wide)]
        o_ref[half, :, pl.ds(place, wide)] = value

        @pl.when(i * group + slots < steps)
        def _():
            for p in range(group):
                for copy in copies(i * group + slots + p, slot + p):
                    copy.start()

        return state

    lax.fori_loop(0, steps // group, step, 0)


def product_call(blocks, places, pieces, s, k, q, cols, operator, near, before):
    rows = operator.shape[0]
    block = cols * q
    t = min(256, q)
    group = max(1, min(512, q) // t)
    slots = group * min(4, rows // (t * group))
    first = near is None
    vmem = pl.BlockSpec(memory_space=pltpu.VMEM)
    args = [places, *pieces]
    specs = [pl.BlockSpec(memory_space=pltpu.SMEM)] + [vmem] * len(pieces)
    if not first:
        args += near
        specs += [vmem] * 3
    if before is not None:
        args += before
        specs += [vmem] * 2
    args.append(operator)
    specs.append(pl.BlockSpec(memory_space=pl.ANY))
    wide = block * len(blocks)
    outs = [
        jax.ShapeDtypeStruct((2, s, rows // 2), f32),
        jax.ShapeDtypeStruct((s, padded(k)), f32),
    ]
    if first:
        outs += [jax.ShapeDtypeStruct((1, wide), f32), jax.ShapeDtypeStruct((1, wide), i32)]
    return pl.pallas_call(
        functools.partial(
            product_kernel, blocks, cols, slots, t, group, s, k, q, first, before is not None
        ),
        in_specs=specs,
        out_specs=[vmem] * len(outs),
        out_shape=outs,
        scratch_shapes=[
            pltpu.VMEM((2 * s, wide), bf16),
            pltpu.VMEM((slots * t, wide), bf16),
            pltpu.SemaphoreType.DMA((slots, len(blocks))),
        ],
        compiler_params=PARAMS,
        cost_estimate=pl.CostEstimate(
            flops=4 * s * rows * wide, bytes_accessed=2 * rows * wide, transcendentals=0
        ),
        name="product",
    )(*args)


def factor(gram):
    n = gram.shape[0]
    panel = 8
    row = lax.broadcasted_iota(i32, (n, 2 * n), 0)
    lane = lax.broadcasted_iota(i32, (n, 2 * n), 1)
    left = jnp.concatenate([gram, jnp.zeros_like(gram)], axis=1) + (lane == row + n).astype(f32)
    found, pivots = [], []
    for at in range(0, n, panel):
        height = n - at
        pivot = jnp.ones((panel, 2 * n), f32)
        for k in range(panel):
            column = jnp.broadcast_to(left[:, at + k : at + k + 1], (height, 2 * n))
            top = column[k : k + 1, :]
            pivot = jnp.where(row[:panel] == k, top, pivot)
            below = jnp.where(row[:height] > k, column, 0.0)
            left = left - below * (left[k : k + 1, :] * (1.0 / top))
        found.append(left[:panel])
        pivots.append(pivot)
        left = left[panel:]
    left, pivot = jnp.concatenate(found, axis=0), jnp.concatenate(pivots, axis=0)
    root = lax.rsqrt(pivot)
    left = left * (root * (1.5 - 0.5 * pivot * root * root))
    row, lane = row[:, :n], lane[:, :n]
    return jnp.where(lane >= row, left[:, :n], 0.0), jnp.where(lane <= row, left[:, n:], 0.0)


def next_kernel(n, n_basis, kind, *refs):
    refs = list(refs)
    sums_ref, new_ref = refs.pop(0), refs.pop(0)
    basis_refs = [refs.pop(0) for _ in range(n_basis)]
    if kind == "last":
        upper_refs = [refs.pop(0) for _ in range(n_basis)]
        coef_refs = [refs.pop(0) for _ in range(n_basis - 1)]
        out_ref, hess_ref, start_ref = refs
        s, q = new_ref.shape
    else:
        image_ref, weight_ref, body_ref = refs.pop(0), refs.pop(0), refs.pop(0)
        image_refs = [refs.pop(0) for _ in range(n_basis)]
        mass_refs = [refs.pop(0) for _ in range(n_basis)]
        v_ref, upper_ref = refs.pop(0), refs.pop(0)
        s, q = v_ref.shape
        if n_basis:
            coef_ref = refs.pop(0)
    k = n_basis * s
    gram = sums_ref[:, k : k + s] / n
    if n_basis:
        coef = sums_ref[:, :k] / n
        gram = gram - dot_exact(coef, coef, 1, 1)
        row = lax.broadcasted_iota(i32, (k, s), 0)
        lane = lax.broadcasted_iota(i32, (k, s), 1)
        shifted = coef.T + jnp.where(row == lane + (k - s), 0.5, 0.0)
        if kind != "last":
            coef_ref[...] = shifted
    upper, inverse = factor(gram)
    if kind != "last":
        upper_ref[...] = upper
    mix = inverse
    if n_basis:
        mix = jnp.concatenate([inverse, -dot_exact(inverse, coef, 1, 0)], axis=1)

    def mixed(values):
        return dot_close(mix, jnp.concatenate(values, axis=0), 1, 0)

    v = mixed([new_ref[...]] + [r[...] for r in basis_refs])
    if kind == "last":
        for b, ref in enumerate(basis_refs):
            out_ref[b * s : (b + 1) * s, :] = ref[...]
        out_ref[n_basis * s :, :] = v
        hess = []
        for b in range(n_basis):
            blocks = [coef_refs[b][...] if b < n_basis - 1 else shifted]
            blocks.append(upper_refs[b + 1][...] if b < n_basis - 1 else upper)
            if b < n_basis - 1:
                blocks.append(jnp.zeros(((n_basis - 1 - b) * s, s), f32))
            hess.append(jnp.concatenate(blocks, axis=0))
        hess_ref[...] = jnp.concatenate(hess, axis=1)
        start_ref[...] = upper_refs[0][...].T
        return
    v_ref[...] = v
    y = mixed([image_ref[...]] + [r[...] for r in image_refs])
    mass = mixed([sums_ref[:, k + s : k + s + BODIES]] + [r[...] for r in mass_refs])
    onehot = onehot_of(body_ref[...])
    weight = weight_ref[...]
    means = mass * (BODIES / n)
    w = y + weight * dot_close(means, onehot, 1, 0)
    stack = [r[...] for r in basis_refs] + [v, w]
    if kind == "middle":
        y_ref, w_ref, mass_ref, mean_ref, payload_ref = refs
        y_ref[...] = y
        mass_ref[...] = mass
        mean_ref[...] = means
        sums = dot_close(w, jnp.concatenate(stack + [onehot * weight], axis=0), 1, 1)
        write_payload(payload_ref, y, sums)
    else:
        w_ref, sums_out = refs
        sums_out[...] = dot_close(w, jnp.concatenate(stack, axis=0), 1, 1)
    w_ref[...] = w


def next_call(n, kind, sums, new, basis, *more):
    s, q = new.shape
    n_basis = len(basis)
    args = [sums, new, *basis, *more]
    if kind == "last":
        outs = [
            jax.ShapeDtypeStruct(((n_basis + 1) * s, q), f32),
            jax.ShapeDtypeStruct(((n_basis + 1) * s, n_basis * s), f32),
            jax.ShapeDtypeStruct((s, s), f32),
        ]
    else:
        outs = [jax.ShapeDtypeStruct((s, q), f32), jax.ShapeDtypeStruct((s, s), f32)]
        if n_basis:
            outs.append(jax.ShapeDtypeStruct((n_basis * s, s), f32))
    if kind == "middle":
        k = (n_basis + 2) * s + BODIES
        outs += [jax.ShapeDtypeStruct((s, q), f32)] * 2
        outs += [jax.ShapeDtypeStruct((s, BODIES), f32)] * 2
        outs.append(jax.ShapeDtypeStruct((s, payload_width(q, k, s)), i16))
    elif kind == "before last":
        outs.append(jax.ShapeDtypeStruct((s, q), f32))
        outs.append(jax.ShapeDtypeStruct((s, (n_basis + 2) * s), f32))
    vmem = pl.BlockSpec(memory_space=pltpu.VMEM)
    return pl.pallas_call(
        functools.partial(next_kernel, n, n_basis, kind),
        in_specs=[vmem] * len(args),
        out_specs=[vmem] * len(outs),
        out_shape=outs,
        compiler_params=PARAMS,
        name="next_block",
    )(*args)


def local(rows, cols, operator, rhs, bodies, weights):
    row_index, col_index = lax.axis_index("row"), lax.axis_index("col")
    s, block = rhs.shape
    n = block * rows
    q = block // cols
    span = rows // cols
    plane, inner = row_index // span, lax.rem(row_index, span)
    places = [(a, g, c) for a in range(cols) for g in range(span) for c in range(cols)]

    def index(a, g, c):
        return (a * span + g) * cols + c

    def permute(value, to):
        return lax.ppermute(value, AXES, [(index(*p), index(*to(*p))) for p in places])

    offsets = jnp.stack(
        [lax.rem(plane - e + cols, cols) * q for e in range(cols)]
        + [lax.rem(inner - d + span, span) * block for d in range(span)]
    ).astype(i32)

    def sum_all(value):
        for bit in [1 << b for b in range(cols.bit_length() - 1)]:
            value = value + permute(value, lambda a, g, c: (a, g, c ^ bit))
        for bit in [1 << b for b in range(span.bit_length() - 1)]:
            value = value + permute(value, lambda a, g, c: (a, g ^ bit, c))
        for bit in [1 << b for b in range(cols.bit_length() - 1)]:
            value = value + permute(value, lambda a, g, c: (a ^ bit, g, c))
        return value

    def scatter_cols(partial, sums):
        core = lax.rem(col_index, 2)
        keep = lax.dynamic_index_in_dim(partial, core, 0, False)
        send = lax.dynamic_index_in_dim(partial, 1 - core, 0, False)
        moved = permute(jnp.concatenate([send, sums], axis=1), lambda a, g, c: (a, g, c ^ 1))
        value = keep + moved[:, : keep.shape[1]]
        sums = sums + moved[:, keep.shape[1] :]
        bit = cols // 2
        while bit > 1:
            half = value.shape[1] // 2
            side = lax.rem(col_index // bit, 2)
            keep = lax.dynamic_slice_in_dim(value, side * half, half, 1)
            send = lax.dynamic_slice_in_dim(value, (1 - side) * half, half, 1)
            level = level_of(send)
            codes = jnp.round(send / jnp.exp2(level * 0.125))
            levels = jnp.broadcast_to(level, (s, LANES))
            codes = jnp.concatenate([codes, levels], axis=1).astype(i16)
            moved, more = [
                permute(v, lambda a, g, c, bit=bit: (a, g, c ^ bit)) for v in (codes, sums)
            ]
            scale = jnp.exp2(moved[:, half : half + 1].astype(f32) * 0.125)
            value = keep + moved[:, :half].astype(f32) * scale
            sums = sums + more
            bit //= 2
        return value, sums

    def image(payload, k, near):
        rounds = [
            permute(payload, lambda a, g, c, d=d: ((c + d) % cols, g, a)) for d in range(cols)
        ]
        mine = jnp.stack(rounds)
        others = [
            permute(mine, lambda a, g, c, d=d: (a, (g + d) % span, c)) for d in range(1, span)
        ]
        first = near is None
        part = product_call(
            (0,), offsets, [mine], s, k, q, cols, operator, None if first else near[0], None
        )
        rest = product_call(
            tuple(range(1, span)),
            offsets,
            others,
            s,
            k,
            q,
            cols,
            operator,
            None if first else near[1],
            part[:2],
        )
        value, sums = scatter_cols(rest[0], rest[1])
        return value, sums, (part[2:], rest[2:])

    new, own_weight, own_body, payload = start_call(
        (col_index * q).astype(i32).reshape(1), rhs, weights[None, :], bodies[None, :], q
    )
    k = s + BODIES
    basis, images, masses, uppers, coefs = [], [], [], [], []
    near = None
    for step in range(STEPS):
        value, sums, found = image(payload, k, near)
        if step == 0:
            around = found
        kind = "middle" if step < STEPS - 1 else "before last"
        out = list(
            next_call(n, kind, sums, new, basis, value, own_weight, own_body, *images, *masses)
        )
        basis.append(out.pop(0))
        uppers.append(out.pop(0))
        if step:
            coefs.append(out.pop(0))
        if kind == "middle":
            y, new, mass, means, payload = out
            images.append(y)
            masses.append(mass)
            near = [[*a, means] for a in around]
            k = (step + 2) * s + BODIES
        else:
            new, sums = out
    return tuple(next_call(n, "last", sum_all(sums), new, basis, *uppers, *coefs))


def solution(mesh):
    rows, cols = mesh.shape["row"], mesh.shape["col"]
    in_specs = (P("row", "col"), P(None, "row"), P("row"), P("row"))
    out_specs = (P(None, ("row", "col")), P(), P())
    return jax.shard_map(
        functools.partial(local, rows, cols),
        mesh=mesh,
        in_specs=in_specs,
        out_specs=out_specs,
        check_vma=False,
    )
```
